32 devices in a mesh: groups: 2 (over x), dp: 4 (over z), tensor: 4 (over y, core).
Axes of the slice: x: 2, y: 2, z: 4, core: 2. Of those that a mesh axis runs over, the one named last changes fastest.
Arguments:
- patches: float32 [16, 256, 6144], P(('groups', 'dp'), None, 'tensor'), parts along dimension 0, may hold values from -60 to 60
- counts: int32 [16], P(('groups', 'dp')), parts along dimension 0, may hold values from 1 to 63, as said below
- ranking: int32 [16, 256], P(('groups', 'dp')), parts along dimension 0, may hold values from 0 to 255, each once within a row
- norm_gain: float32 [6144], P('tensor'), may hold values from 0.1 to 1.9
- expand_weight: bfloat16 [24576, 6144], P(('dp', 'tensor')), may hold values from -0.078125 to 0.078125
- expand_bias: bfloat16 [24576], P(('dp', 'tensor')), may hold values from -4 to 4
- reduce_weight: bfloat16 [24576, 6144], P(('dp', 'tensor')), may hold values from -0.078125 to 0.078125
- reduce_bias: float32 [6144], P('tensor'), may hold values from -4 to 4
Outputs:
- updated: float32 [16, 256, 6144], P(('groups', 'dp'), None, 'tensor'), parts along dimension 0
The draws below stay inside these ranges and needn't reach their ends.
There are 2 independent parts, one for each index of `groups`. The reference program is written for one: setup_inputs(seed, part) draws one part's arguments, and reference() takes and returns one part's arrays. A program takes and returns all parts, laid end to end along the dimension named above; an argument that names none is the same for every part. Nothing has to cross between parts.
Inputs may be any that keep to these rules, and one draw needn't show every extreme that they name: The counts of the 2 images of one index of dp (images b * 2 to (b + 1) * 2 - 1) sum to at most 64; in every draw one such group sums to exactly 64, and some image holds exactly 63.
All inputs are finite; a program needn't handle non-finite values.
Results may differ from the reference program's by a relative error of at most 0.00061.
Values may be sent and summed in bfloat16 or wider, within the bound.
No kernel may reach another device: no remote copies, remote signals or barrier semaphores. Data moves between devices by JAX's collectives and lax.ppermute only.
A program may use at most 128 MiB of HBM per device.

```python
import jax
import jax.numpy as jnp
from jax import lax

D = 6144
FF = 24576
PATCH = 256
IMG_DEV = 2
CAP = 64
IMAGES = 8


def draw_patches(key, part):
    key_base, key_rows, key_cols = jax.random.split(key, 3)
    ramp = 1.0 + 2.0 * jnp.arange(D, dtype=jnp.float32) / D
    cols = jnp.exp(jax.random.uniform(key_cols, (1, 1, D), jnp.float32, jnp.log(0.5), jnp.log(1.5))) * ramp
    base = jnp.clip(jax.random.normal(key_base, (IMAGES, PATCH, D), jnp.float32), -4.0, 4.0)
    rows = jnp.exp(jax.random.uniform(key_rows, (IMAGES, PATCH, 1), jnp.float32, jnp.log(0.3), jnp.log(3.0)))
    return base * rows * cols


def draw_counts(key, part):
    key_total, key_full, key_share = jax.random.split(jax.random.fold_in(key, 17), 3)
    blocks = IMAGES // IMG_DEV
    totals = jax.random.randint(key_total, (blocks,), IMG_DEV, CAP + 1)
    full = jax.random.randint(key_full, (), 0, blocks)
    totals = jnp.where(jnp.arange(blocks) == full, CAP, totals)
    shares = jax.random.randint(key_share, (blocks, IMG_DEV), 1, 100)
    extra = totals - IMG_DEV
    pieces = 1 + extra[:, None] * shares // jnp.sum(shares, axis=1, keepdims=True)
    rest = totals - jnp.sum(pieces, axis=1)
    pieces = pieces.at[:, 0].add(rest)
    lopsided = jnp.where(jnp.arange(IMG_DEV) == 0, CAP - IMG_DEV + 1, 1)
    pieces = jnp.where((jnp.arange(blocks) == full)[:, None], lopsided[None, :], pieces)
    return pieces.reshape(IMAGES).astype(jnp.int32)


def levels(key, extent, cuts, least, high):
    gain, own = 1.0, jax.random.fold_in(key, 6)
    for position, blocks in cuts:
        steps = jnp.exp(jax.random.uniform(jax.random.fold_in(own, position), (blocks,), jnp.float32, least / len(cuts), high / len(cuts)))
        gain = gain * jnp.repeat(steps, extent[position] // blocks).reshape([-1 if axis == position else 1 for axis in range(len(extent))])
    return gain


def noise(rng, dims, spread, most, cuts=(), kind=jnp.bfloat16):
    loudness = levels(rng, dims, cuts, -0.22, 0.18) if cuts else 1.0
    drawn = jax.random.normal(rng, dims, jnp.float32) * spread * loudness
    return jnp.minimum(jnp.maximum(drawn, -most), most).astype(kind)


def setup_inputs(seed: int = 0, part: int = 0) -> dict:
    seeds = jax.random.split(jax.random.key(seed), 9)
    part_keys = jax.random.split(jax.random.fold_in(seeds[8], part), 9)
    return {
        "patches": draw_patches(jax.random.fold_in(jax.random.fold_in(seeds[8], part), 71), part),
        "counts": draw_counts(jax.random.fold_in(jax.random.fold_in(seeds[8], part), 71), part),
        "ranking": jax.vmap(lambda own: jax.random.permutation(own, PATCH))(jax.random.split(part_keys[2], IMAGES)).reshape((IMAGES, PATCH)).astype(jnp.int32),
        "norm_gain": jnp.clip(1.0 + 0.18 * jax.random.normal(seeds[3], (D,), jnp.float32), 0.1, 1.9),
        "expand_weight": noise(seeds[4], (FF, D), D ** -0.5, 0.078125, ((0, 16),)),
        "expand_bias": noise(seeds[5], (FF,), 0.7, 4.0, ((0, 16),)),
        "reduce_weight": noise(seeds[6], (FF, D), (FF // 4) ** -0.5, 0.078125, ((0, 16),)),
        "reduce_bias": noise(seeds[7], (D,), 0.7, 4.0, ((0, 4),), jnp.float32),
    }


def reference(patches, counts, ranking, norm_gain, expand_weight, expand_bias, reduce_weight, reduce_bias):
    chosen = ranking[:, :CAP].astype(jnp.int32)
    live = jnp.arange(CAP, dtype=jnp.int32)[None, :] < counts[:, None]
    rows = jnp.take_along_axis(patches, chosen[:, :, None], axis=1)
    flat = rows.reshape(IMAGES * CAP, D)
    first = lax.optimization_barrier(jnp.sum(flat, axis=1, keepdims=True))
    second = lax.optimization_barrier(jnp.sum(flat * flat, axis=1, keepdims=True))
    mean = first / D
    var = second / D - mean * mean
    normed = ((flat - mean) * lax.rsqrt(var + 1e-06) * norm_gain).astype(jnp.bfloat16)
    pre = lax.dot_general(normed, expand_weight, (((1,), (1,)), ((), ())), preferred_element_type=jnp.float32)
    pre = pre + expand_bias.astype(jnp.float32)
    hidden = jax.nn.gelu(pre, approximate=True).astype(jnp.bfloat16)
    branch = jnp.dot(hidden, reduce_weight, preferred_element_type=jnp.float32)
    update = flat + (branch + reduce_bias)
    update = jnp.where(live.reshape(IMAGES * CAP)[:, None], update, flat).reshape(IMAGES, CAP, D)
    image_index = jnp.arange(IMAGES, dtype=jnp.int32)[:, None]
    return patches.at[image_index, chosen].set(update)
```

```python
import functools

import jax
import jax.numpy as jnp
from jax import lax
from jax.experimental import pallas as pl
from jax.experimental.pallas import tpu as pltpu
from jax.sharding import PartitionSpec as P

CAP = 64
LANES = 128
F32 = jnp.float32
BF16 = jnp.bfloat16
VMEM_LIMIT = 40 * 2**20

whole = pl.BlockSpec(memory_space=pltpu.VMEM)
scalars = pl.BlockSpec(memory_space=pltpu.SMEM)
anywhere = pl.BlockSpec(memory_space=pl.ANY)


def params():
    return pltpu.CompilerParams(vmem_limit_bytes=VMEM_LIMIT)


def slot_source(slot, counts_ref, ranking_ref):
    images = counts_ref.shape[0]
    image, start, end = jnp.int32(0), jnp.int32(0), jnp.int32(0)
    for i in range(images - 1):
        end = end + counts_ref[i]
        past = slot >= end
        image = jnp.where(past, i + 1, image)
        start = jnp.where(past, end, start)
    return image, ranking_ref[image, slot - start]


def gather_kernel(counts_ref, ranking_ref, patches_ref, rows_ref, stats_ref, sem):
    def fetch(slot, carry):
        image, patch = slot_source(slot, counts_ref, ranking_ref)
        pltpu.make_async_copy(
            patches_ref.at[image, pl.ds(patch, 1)], rows_ref.at[pl.ds(slot, 1)], sem
        ).start()
        return carry

    lax.fori_loop(0, CAP, fetch, 0)
    pltpu.make_async_copy(patches_ref.at[0, pl.ds(0, CAP)], rows_ref, sem).wait()
    rows = rows_ref[...]
    first = jnp.sum(rows, axis=1, keepdims=True)
    second = jnp.sum(rows * rows, axis=1, keepdims=True)
    lane = lax.broadcasted_iota(jnp.int32, (CAP, LANES), 1)
    stats_ref[...] = jnp.where(lane < LANES // 2, first, second)


def norm_kernel(width, rows_ref, gain_ref, *refs):
    *stats_refs, out_ref = refs
    stats = stats_refs[0][...]
    for ref in stats_refs[1:]:
        stats = stats + ref[...]
    mean = stats[:, :1] / width
    var = stats[:, LANES - 1 :] / width - mean * mean
    scale = lax.rsqrt(var + 1e-06)
    out_ref[...] = ((rows_ref[...] - mean) * scale * gain_ref[...]).astype(BF16)


def expand_kernel(chunks, groups, index_ref, weight_ref, bias_ref, *refs):
    inputs, (out_ref, rows_ref, total_ref) = refs[:-3], refs[-3:]
    chunk, piece = pl.program_id(0), pl.program_id(1)
    pieces = pl.num_programs(1)
    for c in range(chunks):

        @pl.when(jnp.logical_and(chunk == c, piece == 0))
        def _():
            for g in range(groups):
                block = inputs[c * groups + g]
                rows_ref[:, g * CAP : (g + 1) * CAP] = jnp.stack(
                    jnp.split(block[...], rows_ref.shape[0], axis=1)
                )

    part = lax.dot_general(
        rows_ref[piece], weight_ref[...], (((1,), (1,)), ((), ())), preferred_element_type=F32
    )
    start = jnp.logical_and(chunk == 0, piece == 0)

    @pl.when(start)
    def _():
        total_ref[...] = part

    @pl.when(jnp.logical_not(start))
    def _():
        total_ref[...] += part

    @pl.when(jnp.logical_and(chunk == chunks - 1, piece == pieces - 1))
    def _():
        pre = total_ref[...] + bias_ref[...].astype(F32)
        out_ref[...] = jax.nn.gelu(pre, approximate=True).astype(BF16)


def piece_of(width):
    return 512 if width % 512 == 0 else width


def expand(index, weight, bias, blocks, chunks, groups):
    hidden, width = weight.shape
    chunk_width = width // chunks
    piece = piece_of(chunk_width)
    pieces = chunk_width // piece
    rows = groups * CAP
    return pl.pallas_call(
        functools.partial(expand_kernel, chunks, groups),
        grid_spec=pltpu.PrefetchScalarGridSpec(
            num_scalar_prefetch=1,
            grid=(chunks, pieces),
            in_specs=[
                pl.BlockSpec((hidden, piece), lambda c, p, t: (0, (t[0] ^ c) * pieces + p)),
                whole,
            ]
            + [whole] * len(blocks),
            out_specs=whole,
            scratch_shapes=[
                pltpu.VMEM((pieces, rows, piece), BF16),
                pltpu.VMEM((rows, hidden), F32),
            ],
        ),
        out_shape=jax.ShapeDtypeStruct((rows, hidden), BF16),
        compiler_params=params(),
        cost_estimate=pl.CostEstimate(
            flops=2 * rows * hidden * width,
            bytes_accessed=2 * hidden * width,
            transcendentals=rows * hidden,
        ),
        name="expand",
    )(index, weight, bias, *blocks)


def reduce_kernel(groups, index_ref, hidden_ref, weight_ref, *refs):
    part = jnp.dot(hidden_ref[...], weight_ref[...], preferred_element_type=F32)
    if len(refs) > groups:
        part = part + jnp.concatenate([ref[...] for ref in refs[:groups]], axis=0).astype(F32)
    for g, ref in enumerate(refs[-groups:]):
        ref[...] = part[g * CAP : (g + 1) * CAP].astype(ref.dtype)


def reduce(index, hidden, weight, offset, chunks, groups, received, dtype):
    rows, depth = hidden.shape
    chunk_width = weight.shape[1] // chunks
    piece = piece_of(chunk_width)
    pieces = chunk_width // piece
    block = pl.BlockSpec((CAP, piece), lambda p, t: (0, p))
    return pl.pallas_call(
        functools.partial(reduce_kernel, groups),
        grid_spec=pltpu.PrefetchScalarGridSpec(
            num_scalar_prefetch=1,
            grid=(pieces,),
            in_specs=[
                whole,
                pl.BlockSpec((depth, piece), lambda p, t: (0, (t[0] ^ offset) * pieces + p)),
            ]
            + [block] * len(received),
            out_specs=[block] * groups,
        ),
        out_shape=[jax.ShapeDtypeStruct((CAP, chunk_width), dtype)] * groups,
        compiler_params=params(),
        cost_estimate=pl.CostEstimate(
            flops=2 * rows * depth * chunk_width,
            bytes_accessed=2 * depth * chunk_width,
            transcendentals=0,
        ),
        name="reduce",
    )(index, hidden, weight, *received)


def scatter_kernel(counts_ref, ranking_ref, rows_ref, bias_ref, patches_ref, own_ref, *refs):
    *received, out_ref, new_ref, sem = refs
    branch = own_ref[...]
    for ref in received:
        branch = branch + ref[...].astype(F32)
    live_slots = counts_ref[0]
    for i in range(1, counts_ref.shape[0]):
        live_slots = live_slots + counts_ref[i]
    slot_index = lax.broadcasted_iota(jnp.int32, branch.shape, 0)
    rows = rows_ref[...]
    new_ref[...] = jnp.where(slot_index < live_slots, rows + (branch + bias_ref[...]), rows)

    def put(slot, carry):
        image, patch = slot_source(slot, counts_ref, ranking_ref)
        pltpu.make_async_copy(
            new_ref.at[pl.ds(slot, 1)], out_ref.at[image, pl.ds(patch, 1)], sem
        ).start()
        return carry

    lax.fori_loop(0, CAP, put, 0)
    pltpu.make_async_copy(new_ref, out_ref.at[0, pl.ds(0, CAP)], sem).wait()


def masks(size):
    return [(2 << k) - 1 for k in reversed(range(size.bit_length() - 1))]


def hops(offset, size, unit, axis):
    path = []
    for mask in masks(size):
        if offset & ((mask + 1) // 2):
            path.append((axis, mask * unit))
            offset ^= mask
    return path


def routes(groups, columns):
    found = {}
    for z in range(groups):
        for y in range(columns):
            along, across = hops(z, groups, 1, "dp"), hops(y, columns, 2, "tensor")
            found[z, y] = tuple(across + along) if z == 1 else tuple(along + across)
    return found


def body(
    sizes, patches, counts, ranking, norm_gain, expand_weight, expand_bias, reduce_weight, reduce_bias
):
    groups, parts = sizes["dp"], sizes["tensor"]
    columns = parts // 2
    images, patch_len, width_local = patches.shape
    width = expand_weight.shape[1]
    index = lax.axis_index("tensor").astype(jnp.int32).reshape(1)

    def hop(array, axis, mask):
        return lax.ppermute(array, axis, [(i, i ^ mask) for i in range(sizes[axis])])

    rows, stats = pl.pallas_call(
        gather_kernel,
        in_specs=[scalars, scalars, anywhere],
        out_specs=[whole, whole],
        out_shape=[
            jax.ShapeDtypeStruct((CAP, width_local), F32),
            jax.ShapeDtypeStruct((CAP, LANES), F32),
        ],
        scratch_shapes=[pltpu.SemaphoreType.DMA],
        compiler_params=params(),
        name="gather",
    )(counts, ranking, patches)
    all_stats = [stats] + [hop(stats, "tensor", k) for k in reversed(range(1, parts))]
    normed = pl.pallas_call(
        functools.partial(norm_kernel, width),
        in_specs=[whole] * (2 + parts),
        out_specs=whole,
        out_shape=jax.ShapeDtypeStruct((CAP, width_local), BF16),
        compiler_params=params(),
        name="norm",
    )(rows, norm_gain.reshape(1, -1), *all_stats)

    path_of = routes(groups, columns)
    offset_of = {path: offset for offset, path in path_of.items()}
    by_length = sorted((p for p in offset_of if p), key=len)
    block = {(): normed}
    for path in by_length:
        block[path] = hop(block[path[:-1]], *path[-1])
    inputs = []
    for y in range(columns):
        mine = [block[path_of[z, y]] for z in range(groups)]
        inputs += mine + [hop(b, "tensor", 1) for b in mine]
    hidden = expand(
        index, expand_weight, expand_bias.reshape(1, -1), inputs, parts, groups
    )

    total = {}
    for y in reversed(range(columns)):
        given = reduce(index, hidden, reduce_weight, 2 * y + 1, parts, groups, [], BF16)
        received = [hop(g, "tensor", 1) for g in given]
        kept = reduce(index, hidden, reduce_weight, 2 * y, parts, groups, received, F32)
        for z in range(groups):
            total[path_of[z, y]] = kept[z]
    arrived = []
    for path in reversed(by_length):
        got = hop(total[path].astype(BF16), *path[-1])
        if path[:-1]:
            total[path[:-1]] = total[path[:-1]] + got.astype(F32)
        else:
            arrived.append(got)

    return pl.pallas_call(
        scatter_kernel,
        in_specs=[scalars, scalars, whole, whole, anywhere, whole] + [whole] * len(arrived),
        out_specs=anywhere,
        out_shape=jax.ShapeDtypeStruct(patches.shape, F32),
        scratch_shapes=[pltpu.VMEM((CAP, width_local), F32), pltpu.SemaphoreType.DMA],
        input_output_aliases={4: 0},
        compiler_params=params(),
        name="scatter",
    )(counts, ranking, rows, reduce_bias.reshape(1, -1), patches, total[()], *arrived)


def solution(mesh):
    placed = (
        P(("groups", "dp"), None, "tensor"),
        P(("groups", "dp")),
        P(("groups", "dp"), None),
        P("tensor"),
        P(("dp", "tensor"), None),
        P(("dp", "tensor")),
        P(("dp", "tensor"), None),
        P("tensor"),
    )
    return jax.shard_map(
        functools.partial(body, dict(mesh.shape)),
        mesh=mesh,
        in_specs=placed,
        out_specs=P(("groups", "dp"), None, "tensor"),
        check_vma=False,
    )
```

```python
import functools

import jax
import jax.numpy as jnp
from jax import lax
from jax.experimental import pallas as pl
from jax.experimental.pallas import tpu as pltpu
from jax.sharding import PartitionSpec as P

CAP = 64
LANES = 128
F32 = jnp.float32
BF16 = jnp.bfloat16

whole = pl.BlockSpec(memory_space=pltpu.VMEM)
scalars = pl.BlockSpec(memory_space=pltpu.SMEM)
outside = pl.BlockSpec(memory_space=pltpu.HBM)


def params(mib=6):
    return pltpu.CompilerParams(vmem_limit_bytes=mib * 2**20)


def slot_source(slot, counts_ref, ranking_ref):
    images = counts_ref.shape[0]
    image, start, end = jnp.int32(0), jnp.int32(0), jnp.int32(0)
    for i in range(images - 1):
        end = end + counts_ref[i]
        past = slot >= end
        image = jnp.where(past, i + 1, image)
        start = jnp.where(past, end, start)
    return image, ranking_ref[image, slot - start]


def gather_kernel(counts_ref, ranking_ref, patches_ref, *refs):
    *_, rows_ref, stats_ref, sem = refs
    def fetch(slot, carry):
        image, patch = slot_source(slot, counts_ref, ranking_ref)
        pltpu.make_async_copy(
            patches_ref.at[image, pl.ds(patch, 1)], rows_ref.at[pl.ds(slot, 1)], sem
        ).start()
        return carry

    lax.fori_loop(0, CAP, fetch, 0)
    pltpu.make_async_copy(patches_ref.at[0, pl.ds(0, CAP)], rows_ref, sem).wait()
    rows = rows_ref[...]
    first = jnp.sum(rows, axis=1, keepdims=True)
    second = jnp.sum(rows * rows, axis=1, keepdims=True)
    lane = lax.broadcasted_iota(jnp.int32, (CAP, LANES), 1)
    stats_ref[...] = jnp.where(lane < LANES // 2, first, second)


def load_kernel(weight_ref, after_ref, *refs):
    *more, sems = refs
    if len(more) == 3:
        patches_ref, out_ref, copy_ref = more
    else:
        [out_ref] = more
    count = sems.shape[0] - 1
    share = weight_ref.shape[0] // count
    copies = [
        pltpu.make_async_copy(
            weight_ref.at[pl.ds(i * share, share)], out_ref.at[pl.ds(i * share, share)], sems.at[i]
        )
        for i in range(count)
    ]
    if len(more) == 3:
        copies.append(pltpu.make_async_copy(patches_ref, copy_ref, sems.at[count]))
    for copy in copies:
        copy.start()
    for copy in copies:
        copy.wait()


def load(weight, after, mib, patches=None):
    shapes = [pltpu.VMEM(weight.shape, weight.dtype)]
    size = 2 * weight.size * weight.dtype.itemsize
    args, specs = [weight, after], [whole]
    if patches is not None:
        args.append(patches)
        shapes.append(pltpu.HBM(patches.shape, patches.dtype))
        specs.append(outside)
    return pl.pallas_call(
        load_kernel,
        in_specs=[outside] * len(args),
        out_specs=specs,
        out_shape=shapes,
        scratch_shapes=[pltpu.SemaphoreType.DMA((5,))],
        compiler_params=params(mib),
        cost_estimate=pl.CostEstimate(flops=0, bytes_accessed=size, transcendentals=0),
        name="load",
    )(*args)


def pass_kernel(block_ref, after_ref, out_ref):
    pass


def pass_on(block, after):
    return pl.pallas_call(
        pass_kernel,
        in_specs=[outside, whole],
        out_specs=outside,
        out_shape=jax.ShapeDtypeStruct(block.shape, block.dtype),
        input_output_aliases={0: 0},
        compiler_params=params(1),
        name="pass_on",
    )(block, after)


def norm_kernel(width, rows_ref, gain_ref, after_ref, *refs):
    *stats_refs, out_ref = refs
    stats = stats_refs[0][...]
    for ref in stats_refs[1:]:
        stats = stats + ref[...]
    mean = stats[:, :1] / width
    var = stats[:, LANES - 1 :] / width - mean * mean
    scale = lax.rsqrt(var + 1e-06)
    out_ref[...] = ((rows_ref[...] - mean) * scale * gain_ref[...]).astype(BF16)


def expand_kernel(first, chunks, groups, last, weight_ref, *refs):
    refs = list(refs)
    total_in = refs.pop(0) if first else None
    bias_ref = refs.pop(0) if last else None
    count = chunks * groups
    inputs, refs = refs[:count], refs[count:]
    out_ref = refs.pop(0)
    rows_ref, sems = refs[:2]
    refs = refs[2:]
    total_ref = refs.pop(0) if last else out_ref
    hidden = weight_ref.shape[0]
    width = rows_ref.shape[2]
    tile = piece_of(hidden)

    def fetch(c, g):
        return pltpu.make_async_copy(
            inputs[c * groups + g], rows_ref.at[c, pl.ds(g * CAP, CAP)], sems.at[c, g]
        )

    for c in range(chunks):
        for g in range(groups):
            fetch(c, g).start()
    for c in range(chunks):
        for g in range(groups):
            fetch(c, g).wait()
        column = pl.multiple_of((lax.axis_index("tensor") ^ (first + c)) * width, width)
        for f in range(hidden // tile):
            part = lax.dot_general(
                rows_ref[c],
                weight_ref[f * tile : (f + 1) * tile, pl.ds(column, width)],
                (((1,), (1,)), ((), ())),
                preferred_element_type=F32,
            )
            tiles = slice(f * tile, (f + 1) * tile)
            if c > 0:
                part = part + total_ref[:, tiles]
            elif first:
                part = part + total_in[:, tiles]
            if last and c == chunks - 1:
                pre = part + bias_ref[:, tiles].astype(F32)
                out_ref[:, tiles] = jax.nn.gelu(pre, approximate=True).astype(BF16)
            else:
                total_ref[:, tiles] = part


def piece_of(width):
    return 512 if width % 512 == 0 else width


def expand(weight, first, total, bias, blocks, groups):
    hidden, width = weight.shape
    chunks = len(blocks) // groups
    chunk_width = blocks[0].shape[1]
    rows = groups * CAP
    last = bias is not None
    args, specs = [weight], [whole]
    scratch = [
        pltpu.VMEM((chunks, rows, chunk_width), BF16),
        pltpu.SemaphoreType.DMA((chunks, groups)),
    ]
    if first:
        args.append(total)
        specs.append(whole)
    if last:
        args.append(bias)
        specs.append(whole)
        scratch.append(pltpu.VMEM((rows, hidden), F32))
    return pl.pallas_call(
        functools.partial(expand_kernel, first, chunks, groups, last),
        in_specs=specs + [outside if first or i else whole for i in range(len(blocks))],
        out_specs=whole,
        out_shape=jax.ShapeDtypeStruct((rows, hidden), BF16 if last else F32),
        scratch_shapes=scratch,
        compiler_params=params(),
        cost_estimate=pl.CostEstimate(
            flops=2 * rows * hidden * chunk_width * chunks,
            bytes_accessed=2 * rows * chunk_width * chunks,
            transcendentals=0,
        ),
        name="expand",
    )(*args, *blocks)


def reduce_kernel(groups, offset, hidden_ref, weight_ref, *refs):
    width = refs[-1].shape[1]
    tile = piece_of(width)
    column = pl.multiple_of((lax.axis_index("tensor") ^ offset) * width, width)
    for n in range(width // tile):
        tiles = slice(n * tile, (n + 1) * tile)
        part = jnp.dot(
            hidden_ref[...],
            weight_ref[:, pl.ds(pl.multiple_of(column + n * tile, LANES), tile)],
            preferred_element_type=F32,
        )
        for g, ref in enumerate(refs[-groups:]):
            piece = part[g * CAP : (g + 1) * CAP]
            if len(refs) > groups:
                piece = piece + refs[g][:, tiles].astype(F32)
            ref[:, tiles] = piece.astype(ref.dtype)


def reduce(hidden, weight, offset, chunks, groups, received, dtypes):
    rows, depth = hidden.shape
    chunk_width = weight.shape[1] // chunks
    return pl.pallas_call(
        functools.partial(reduce_kernel, groups, offset),
        in_specs=[whole, whole] + [whole] * len(received),
        out_specs=[whole] * groups,
        out_shape=[jax.ShapeDtypeStruct((CAP, chunk_width), dtype) for dtype in dtypes],
        compiler_params=params(),
        cost_estimate=pl.CostEstimate(
            flops=2 * rows * depth * chunk_width,
            bytes_accessed=2 * rows * chunk_width,
            transcendentals=0,
        ),
        name="reduce",
    )(hidden, weight, *received)


def add_kernel(*refs):
    *given, out_ref = refs
    value = given[0][...]
    for ref in given[1:]:
        value = value + ref[...].astype(F32)
    out_ref[...] = value.astype(out_ref.dtype)


def add(parts):
    if len(parts) == 1:
        return parts[0]
    return pl.pallas_call(
        add_kernel,
        in_specs=[whole] * len(parts),
        out_specs=whole,
        out_shape=pltpu.VMEM(parts[0].shape, BF16),
        compiler_params=params(4),
        name="add",
    )(*parts)


def scatter_kernel(counts_ref, ranking_ref, rows_ref, bias_ref, patches_ref, own_ref, *refs):
    *received, out_ref, new_ref, sem = refs
    branch = own_ref[...]
    for ref in received:
        branch = branch + ref[...].astype(F32)
    live_slots = counts_ref[0]
    for i in range(1, counts_ref.shape[0]):
        live_slots = live_slots + counts_ref[i]
    slot_index = lax.broadcasted_iota(jnp.int32, branch.shape, 0)
    rows = rows_ref[...]
    new_ref[...] = jnp.where(slot_index < live_slots, rows + (branch + bias_ref[...]), rows)

    def put(slot, carry):
        image, patch = slot_source(slot, counts_ref, ranking_ref)
        pltpu.make_async_copy(
            new_ref.at[pl.ds(slot, 1)], out_ref.at[image, pl.ds(patch, 1)], sem
        ).start()
        return carry

    lax.fori_loop(0, CAP, put, 0)
    pltpu.make_async_copy(new_ref, out_ref.at[0, pl.ds(0, CAP)], sem).wait()


def masks(size):
    return [(2 << k) - 1 for k in reversed(range(size.bit_length() - 1))]


def hops(offset, size, unit, axis):
    path = []
    for mask in masks(size):
        if offset & ((mask + 1) // 2):
            path.append((axis, mask * unit))
            offset ^= mask
    return path


def routes(groups, columns):
    found = {}
    for z in range(groups):
        for y in range(columns):
            along, across = hops(z, groups, 1, "dp"), hops(y, columns, 2, "tensor")
            found[z, y] = tuple(across + along) if z == 1 else tuple(along + across)
    return found


def body(
    sizes, patches, counts, ranking, norm_gain, expand_weight, expand_bias, reduce_weight, reduce_bias
):
    groups, parts = sizes["dp"], sizes["tensor"]
    columns = parts // 2
    images, patch_len, width_local = patches.shape
    width = expand_weight.shape[1]
    patches, expand_weight, reduce_weight = (
        pltpu.with_memory_space_constraint(a, pltpu.HBM)
        for a in (patches, expand_weight, reduce_weight)
    )
    gain, bias, last_bias = (
        a.reshape(1, -1) for a in (norm_gain, expand_bias, reduce_bias)
    )

    def hop(array, axis, mask):
        return lax.ppermute(array, axis, [(i, i ^ mask) for i in range(sizes[axis])])

    rows, stats = pl.pallas_call(
        gather_kernel,
        in_specs=[scalars, scalars, outside] + [pl.BlockSpec(memory_space=pl.ANY)] * 3,
        out_specs=[whole, whole],
        out_shape=[
            pltpu.VMEM((CAP, width_local), F32),
            pltpu.VMEM((CAP, LANES), F32),
        ],
        scratch_shapes=[pltpu.SemaphoreType.DMA],
        compiler_params=params(),
        name="gather",
    )(counts, ranking, patches, gain, bias, last_bias)
    expand_weight, copied = load(expand_weight, stats, 8, patches)
    expand_weight = pltpu.with_memory_space_constraint(expand_weight, pltpu.VMEM)
    all_stats = [stats] + [hop(stats, "tensor", k) for k in reversed(range(1, parts))]
    normed = pl.pallas_call(
        functools.partial(norm_kernel, width),
        in_specs=[whole] * (3 + parts),
        out_specs=whole,
        out_shape=jax.ShapeDtypeStruct((CAP, width_local), BF16),
        compiler_params=params(),
        name="norm",
    )(rows, gain, expand_weight, *all_stats)

    [reduce_weight] = load(reduce_weight, normed, 8)
    reduce_weight = pltpu.with_memory_space_constraint(reduce_weight, pltpu.VMEM)
    path_of = routes(groups, columns)
    offset_of = {path: offset for offset, path in path_of.items()}
    by_length = sorted((p for p in offset_of if p), key=len)
    block = {(): normed}
    for path in by_length:
        block[path] = hop(block[path[:-1]], *path[-1])
        if path == (("dp", groups - 1),):
            block[path] = pass_on(block[path], reduce_weight)
    running = None
    for y in range(columns):
        mine = [block[path_of[z, y]] for z in range(groups)]
        inputs = mine + [hop(b, "tensor", 1) for b in mine]
        running = expand(
            expand_weight,
            2 * y,
            running,
            bias if y == columns - 1 else None,
            inputs,
            groups,
        )
    hidden = running

    total = {}
    for y in reversed(range(columns)):
        given = reduce(
            hidden, reduce_weight, 2 * y + 1, parts, groups, [], [BF16] * groups
        )
        received = [hop(g, "tensor", 1) for g in given]
        paths = [path_of[z, y] for z in range(groups)]
        parents = {p[:-1] for p in by_length}
        dtypes = [F32 if p in parents else BF16 for p in paths]
        kept = reduce(hidden, reduce_weight, 2 * y, parts, groups, received, dtypes)
        total.update(zip(paths, kept))
    terms = {path: [value] for path, value in total.items()}
    for path in reversed(by_length):
        terms[path[:-1]].append(hop(add(terms[path]), *path[-1]))
    own, *arrived = terms[()]

    return pl.pallas_call(
        scatter_kernel,
        in_specs=[scalars, scalars, whole, whole, outside, whole] + [whole] * len(arrived),
        out_specs=outside,
        out_shape=jax.ShapeDtypeStruct(patches.shape, F32),
        scratch_shapes=[pltpu.VMEM((CAP, width_local), F32), pltpu.SemaphoreType.DMA],
        input_output_aliases={4: 0},
        compiler_params=params(),
        name="scatter",
    )(counts, ranking, rows, last_bias, copied, own, *arrived)


def solution(mesh):
    placed = (
        P(("groups", "dp"), None, "tensor"),
        P(("groups", "dp")),
        P(("groups", "dp"), None),
        P("tensor"),
        P(("dp", "tensor"), None),
        P(("dp", "tensor")),
        P(("dp", "tensor"), None),
        P("tensor"),
    )
    return jax.shard_map(
        functools.partial(body, dict(mesh.shape)),
        mesh=mesh,
        in_specs=placed,
        out_specs=P(("groups", "dp"), None, "tensor"),
        check_vma=False,
    )
```

```python
import functools

import jax
import jax.numpy as jnp
from jax import lax
from jax.experimental import pallas as pl
from jax.experimental.pallas import tpu as pltpu
from jax.sharding import PartitionSpec as P

CAP = 64
LANES = 128
PARTS = 2
F32 = jnp.float32
BF16 = jnp.bfloat16

whole = pl.BlockSpec(memory_space=pltpu.VMEM)
scalars = pl.BlockSpec(memory_space=pltpu.SMEM)
outside = pl.BlockSpec(memory_space=pltpu.HBM)


def params(mib=6):
    return pltpu.CompilerParams(vmem_limit_bytes=mib * 2**20)


def slot_source(slot, counts_ref, ranking_ref):
    images = counts_ref.shape[0]
    image, start, end = jnp.int32(0), jnp.int32(0), jnp.int32(0)
    for i in range(images - 1):
        end = end + counts_ref[i]
        past = slot >= end
        image = jnp.where(past, i + 1, image)
        start = jnp.where(past, end, start)
    return image, ranking_ref[image, slot - start]


def gather_kernel(
    counts_any, ranking_any, patches_ref, rows_ref, stats_ref, counts_ref, ranking_ref, sem, sems
):
    copies = [
        pltpu.make_async_copy(counts_any, counts_ref, sems.at[0]),
        pltpu.make_async_copy(ranking_any, ranking_ref, sems.at[1]),
    ]
    for copy in copies:
        copy.start()
    for copy in copies:
        copy.wait()

    def fetch(slot, carry):
        image, patch = slot_source(slot, counts_ref, ranking_ref)
        pltpu.make_async_copy(
            patches_ref.at[image, pl.ds(patch, 1)], rows_ref.at[pl.ds(slot, 1)], sem
        ).start()
        return carry

    lax.fori_loop(0, CAP, fetch, 0)
    pltpu.make_async_copy(patches_ref.at[0, pl.ds(0, CAP)], rows_ref, sem).wait()
    rows = rows_ref[...]
    first = jnp.sum(rows, axis=1, keepdims=True)
    second = jnp.sum(rows * rows, axis=1, keepdims=True)
    lane = lax.broadcasted_iota(jnp.int32, (CAP, LANES), 1)
    stats_ref[...] = jnp.where(lane < LANES // 2, first, second)


def load_kernel(parts, after_ref, *refs):
    weights, refs, sems = refs[: len(parts)], refs[len(parts) : -1], refs[-1]
    copies = []
    for w, part in enumerate(parts):
        share = refs[w].shape[0] // sems.shape[1]
        for i in range(sems.shape[1]):
            row = part * refs[w].shape[0] + i * share
            copies.append(
                pltpu.make_async_copy(
                    weights[w].at[pl.ds(row, share)],
                    refs[w].at[pl.ds(i * share, share)],
                    sems.at[w, i],
                )
            )
    for copy in copies:
        copy.start()
    for copy in copies:
        copy.wait()


def load(after, *shares):
    weights = [weight for weight, _ in shares]
    shapes = [pltpu.VMEM((w.shape[0] // PARTS, w.shape[1]), w.dtype) for w in weights]
    size = sum(w.size * w.dtype.itemsize // PARTS for w in weights)
    loaded = pl.pallas_call(
        functools.partial(load_kernel, tuple(part for _, part in shares)),
        in_specs=[pl.BlockSpec(memory_space=pl.ANY)] + [outside] * len(shares),
        out_specs=[whole] * len(shares),
        out_shape=shapes,
        scratch_shapes=[pltpu.SemaphoreType.DMA((len(shares), 2))],
        compiler_params=params(),
        cost_estimate=pl.CostEstimate(flops=0, bytes_accessed=2 * size, transcendentals=0),
        name="load",
    )(after, *weights)
    return [pltpu.with_memory_space_constraint(w, pltpu.VMEM) for w in loaded]


def copy_kernel(patches_ref, after_ref, out_ref, held_ref, sems):
    images = patches_ref.shape[0]
    inward = [
        pltpu.make_async_copy(patches_ref.at[i], held_ref.at[i], sems.at[0, i])
        for i in range(images)
    ]
    outward = [
        pltpu.make_async_copy(held_ref.at[i], out_ref.at[i], sems.at[1, i]) for i in range(images)
    ]
    for copy in inward:
        copy.start()
    for i in range(images):
        inward[i].wait()
        outward[i].start()
    for copy in outward:
        copy.wait()


def copy(patches, after):
    return pl.pallas_call(
        copy_kernel,
        in_specs=[outside, pl.BlockSpec(memory_space=pl.ANY)],
        out_specs=outside,
        out_shape=pltpu.HBM(patches.shape, patches.dtype),
        scratch_shapes=[
            pltpu.VMEM(patches.shape, patches.dtype),
            pltpu.SemaphoreType.DMA((2, patches.shape[0])),
        ],
        compiler_params=params(),
        cost_estimate=pl.CostEstimate(
            flops=0, bytes_accessed=2 * patches.size * 4, transcendentals=0
        ),
        name="copy",
    )(patches, after)


def pass_kernel(*refs):
    pass


def pass_on(block, after):
    return pl.pallas_call(
        pass_kernel,
        in_specs=[whole] * (1 + len(after)),
        out_specs=whole,
        out_shape=pltpu.VMEM(block.shape, block.dtype),
        input_output_aliases={0: 0},
        compiler_params=params(1),
        name="pass_on",
    )(block, *after)


def norm_kernel(width, rows_ref, gain_ref, after_ref, *refs):
    *stats_refs, out_ref = refs
    stats = stats_refs[0][...]
    for ref in stats_refs[1:]:
        stats = stats + ref[...]
    mean = stats[:, :1] / width
    var = stats[:, LANES - 1 :] / width - mean * mean
    scale = lax.rsqrt(var + 1e-06)
    out_ref[...] = ((rows_ref[...] - mean) * scale * gain_ref[...].reshape(1, -1)).astype(BF16)


def tile_of(width, most):
    return most if width % most == 0 else width


def expand_kernel(first, chunks, groups, last, *refs):
    refs = list(refs)
    weights, refs = refs[:PARTS], refs[PARTS:]
    total_in = refs.pop(0) if first else None
    bias_ref = refs.pop(0) if last else None
    inputs, refs = refs[: chunks * groups], refs[chunks * groups :]
    out_ref, rows_ref = refs[:2]
    total_ref = refs[2] if last else out_ref
    height, width = weights[0].shape[0], rows_ref.shape[1]
    tile = tile_of(height, 256)
    for c in range(chunks):
        for g in range(groups):
            rows_ref[g * CAP : (g + 1) * CAP, :] = inputs[c * groups + g][...]
        column = pl.multiple_of((lax.axis_index("tensor") ^ (first + c)) * width, width)
        for f in range(PARTS * height // tile):
            weight_ref, row = weights[f * tile // height], f * tile % height
            part = lax.dot_general(
                rows_ref[...],
                weight_ref[row : row + tile, pl.ds(column, width)],
                (((1,), (1,)), ((), ())),
                preferred_element_type=F32,
            )
            tiles = slice(f * tile, (f + 1) * tile)
            if c > 0:
                part = part + total_ref[:, tiles]
            elif first:
                part = part + total_in[:, tiles]
            if last and c == chunks - 1:
                pre = part + bias_ref[tiles].reshape(1, -1).astype(F32)
                out_ref[:, tiles] = jax.nn.gelu(pre, approximate=True).astype(BF16)
            else:
                total_ref[:, tiles] = part


def expand(weights, first, total, bias, blocks, groups):
    hidden = PARTS * weights[0].shape[0]
    chunks = len(blocks) // groups
    chunk_width = blocks[0].shape[1]
    rows = groups * CAP
    last = bias is not None
    args = [*weights]
    scratch = [pltpu.VMEM((rows, chunk_width), BF16)]
    if first:
        args.append(total)
    if last:
        args.append(bias)
        scratch.append(pltpu.VMEM((rows, hidden), F32))
    args += blocks
    return pl.pallas_call(
        functools.partial(expand_kernel, first, chunks, groups, last),
        in_specs=[whole] * len(args),
        out_specs=whole,
        out_shape=pltpu.VMEM((rows, hidden), BF16 if last else F32),
        scratch_shapes=scratch,
        compiler_params=params(),
        cost_estimate=pl.CostEstimate(
            flops=2 * rows * hidden * chunk_width * chunks,
            bytes_accessed=2 * rows * chunk_width * chunks,
            transcendentals=0,
        ),
        name="expand",
    )(*args)


def reduce_kernel(groups, start, offset, hidden_ref, *refs):
    weights, refs = refs[:PARTS], refs[PARTS:]
    height, width = weights[0].shape[0], refs[-1].shape[1]
    tile = tile_of(width, 512)
    column = pl.multiple_of((lax.axis_index("tensor") ^ offset) * width, width)
    for n in range(width // tile):
        tiles = slice(n * tile, (n + 1) * tile)
        columns = pl.ds(pl.multiple_of(column + n * tile, LANES), tile)
        part = None
        for i, ref in enumerate(weights):
            term = jnp.dot(
                hidden_ref[start * CAP : (start + groups) * CAP, i * height : (i + 1) * height],
                ref[:, columns],
                preferred_element_type=F32,
            )
            part = term if part is None else part + term
        for g, ref in enumerate(refs[-groups:]):
            piece = part[g * CAP : (g + 1) * CAP]
            if len(refs) > groups:
                piece = piece + refs[g][:, tiles].astype(F32)
            ref[:, tiles] = piece.astype(ref.dtype)


def reduce(hidden, weights, offset, chunks, offsets, received, dtypes):
    groups, depth = len(offsets), hidden.shape[1]
    rows = groups * CAP
    chunk_width = weights[0].shape[1] // chunks
    return pl.pallas_call(
        functools.partial(reduce_kernel, groups, offsets[0], offset),
        in_specs=[whole] * (1 + PARTS + len(received)),
        out_specs=[whole] * groups,
        out_shape=[pltpu.VMEM((CAP, chunk_width), dtype) for dtype in dtypes],
        compiler_params=params(),
        cost_estimate=pl.CostEstimate(
            flops=2 * rows * depth * chunk_width,
            bytes_accessed=2 * rows * chunk_width,
            transcendentals=0,
        ),
        name="reduce",
    )(hidden, *weights, *received)


def add_kernel(*refs):
    *given, out_ref = refs
    value = given[0][...]
    for ref in given[1:]:
        value = value + ref[...].astype(F32)
    out_ref[...] = value.astype(out_ref.dtype)


def add(parts):
    if len(parts) == 1:
        return parts[0]
    return pl.pallas_call(
        add_kernel,
        in_specs=[whole] * len(parts),
        out_specs=whole,
        out_shape=pltpu.VMEM(parts[0].shape, BF16),
        compiler_params=params(4),
        name="add",
    )(*parts)


def scatter_kernel(counts_ref, ranking_ref, rows_ref, bias_ref, patches_ref, own_ref, *refs):
    *received, out_ref, new_ref, sem = refs
    branch = own_ref[...]
    for ref in received:
        branch = branch + ref[...].astype(F32)
    live_slots = counts_ref[0]
    for i in range(1, counts_ref.shape[0]):
        live_slots = live_slots + counts_ref[i]
    slot_index = lax.broadcasted_iota(jnp.int32, branch.shape, 0)
    rows = rows_ref[...]
    new_ref[...] = jnp.where(slot_index < live_slots, rows + (branch + bias_ref[...].reshape(1, -1)), rows)

    def put(slot, carry):
        image, patch = slot_source(slot, counts_ref, ranking_ref)
        pltpu.make_async_copy(
            new_ref.at[pl.ds(slot, 1)], out_ref.at[image, pl.ds(patch, 1)], sem
        ).start()
        return carry

    lax.fori_loop(0, CAP, put, 0)
    pltpu.make_async_copy(new_ref, out_ref.at[0, pl.ds(0, CAP)], sem).wait()


def masks(size):
    return [(2 << k) - 1 for k in reversed(range(size.bit_length() - 1))]


def hops(offset, size, unit, axis):
    path = []
    for mask in masks(size):
        if offset & ((mask + 1) // 2):
            path.append((axis, mask * unit))
            offset ^= mask
    return path


def routes(groups, columns):
    found = {}
    for z in range(groups):
        for y in range(columns):
            along, across = hops(z, groups, 1, "dp"), hops(y, columns, 2, "tensor")
            found[z, y] = tuple(across + along) if z == 1 else tuple(along + across)
    return found


def body(
    sizes, patches, counts, ranking, norm_gain, expand_weight, expand_bias, reduce_weight, reduce_bias
):
    groups, parts = sizes["dp"], sizes["tensor"]
    columns = parts // 2
    images, patch_len, width_local = patches.shape
    width = expand_weight.shape[1]
    patches, counts, ranking, expand_weight, reduce_weight = (
        pltpu.with_memory_space_constraint(a, pltpu.HBM)
        for a in (patches, counts, ranking, expand_weight, reduce_weight)
    )

    def hop(array, axis, mask):
        return lax.ppermute(array, axis, [(i, i ^ mask) for i in range(sizes[axis])])

    rows, stats = pl.pallas_call(
        gather_kernel,
        in_specs=[outside] * 3,
        out_specs=[whole, whole],
        out_shape=[
            pltpu.VMEM((CAP, width_local), F32),
            pltpu.VMEM((CAP, LANES), F32),
        ],
        scratch_shapes=[
            pltpu.SMEM(counts.shape, jnp.int32),
            pltpu.SMEM(ranking.shape, jnp.int32),
            pltpu.SemaphoreType.DMA,
            pltpu.SemaphoreType.DMA((2,)),
        ],
        compiler_params=params(),
        name="gather",
    )(counts, ranking, patches)
    [early] = load(stats, (expand_weight, 0))
    all_stats = [stats] + [hop(stats, "tensor", k) for k in reversed(range(1, parts))]
    normed = pl.pallas_call(
        functools.partial(norm_kernel, width),
        in_specs=[whole] * (3 + parts),
        out_specs=whole,
        out_shape=jax.ShapeDtypeStruct((CAP, width_local), BF16),
        compiler_params=params(),
        name="norm",
    )(rows, norm_gain, early, *all_stats)

    path_of = routes(groups, columns)
    offset_of = {path: offset for offset, path in path_of.items()}
    by_length = sorted((p for p in offset_of if p), key=len)
    late = [(w, i) for w in (expand_weight, reduce_weight) for i in range(1, PARTS)]
    late = load(normed, *late)
    expand_weights = [early] + late[: PARTS - 1]
    half, last = groups // 2, columns - 1
    block = {(): normed}
    far, mid = path_of[groups - 1, 0], path_of[half, 0]
    block[far] = hop(normed, *far[0])
    for path in by_length:
        if len(path) == 1 and path != far:
            block[path] = hop(normed, *path[0])
    near = [block[p] for p in (path_of[0, y] for y in range(1, columns)) if p in block]
    block[far] = pass_on(block[far], late + near)
    block[mid] = hop(block[far], *mid[-1])
    for y in range(1, columns):
        path = path_of[groups - 1, y]
        if path[:-1] == far:
            block[path] = hop(block[far], *path[-1])
    [reduce_early] = load(block[far], (reduce_weight, 0))
    reduce_weights = [reduce_early] + late[PARTS - 1 :]
    block[mid] = pass_on(
        block[mid],
        [reduce_early] + [block[p] for p in by_length if p[:-1] == far and p != mid and p in block],
    )
    for path in by_length:
        if path not in block:
            block[path] = hop(block[path[:-1]], *path[-1])

    running = None
    for y in range(columns):
        mine = [block[path_of[z, y]] for z in range(groups)]
        if y:
            mine[half] = pass_on(mine[half], [running])
        inputs = mine + [hop(b, "tensor", 1) for b in mine]
        bias = expand_bias if y == last else None
        running = expand(expand_weights, 2 * y, running, bias, inputs, groups)

    terms = {}
    parents = {p[:-1] for p in by_length}
    for y in reversed(range(columns)):
        ranges = (range(half, groups), range(half))
        received = []
        for offsets in ranges:
            given = reduce(
                running, reduce_weights, 2 * y + 1, parts, offsets, [], [BF16] * half
            )
            received.append([hop(g, "tensor", 1) for g in given])
        for offsets, got in zip(ranges, received):
            paths = [path_of[z, y] for z in offsets]
            dtypes = [F32 if p in parents else BF16 for p in paths]
            kept = reduce(running, reduce_weights, 2 * y, parts, offsets, got, dtypes)
            terms.update((p, [k]) for p, k in zip(paths, kept))
    copied = copy(patches, terms[()][0])
    order = list(reversed(by_length))
    for path in order:
        value = add(terms[path])
        if path != order[0] and path[-1] == order[0][-1]:
            value = pass_on(value, [got])
        sent = hop(value, *path[-1])
        if path == order[0]:
            got = sent
        terms[path[:-1]].append(sent)
    own, *arrived = terms[()]

    return pl.pallas_call(
        scatter_kernel,
        in_specs=[scalars, scalars, whole, whole, outside, whole] + [whole] * len(arrived),
        out_specs=outside,
        out_shape=jax.ShapeDtypeStruct(patches.shape, F32),
        scratch_shapes=[pltpu.VMEM((CAP, width_local), F32), pltpu.SemaphoreType.DMA],
        input_output_aliases={4: 0},
        compiler_params=params(),
        name="scatter",
    )(counts, ranking, rows, reduce_bias, copied, own, *arrived)


def solution(mesh):
    placed = (
        P(("groups", "dp"), None, "tensor"),
        P(("groups", "dp")),
        P(("groups", "dp"), None),
        P("tensor"),
        P(("dp", "tensor"), None),
        P(("dp", "tensor")),
        P(("dp", "tensor"), None),
        P("tensor"),
    )
    return jax.shard_map(
        functools.partial(body, dict(mesh.shape)),
        mesh=mesh,
        in_specs=placed,
        out_specs=P(("groups", "dp"), None, "tensor"),
        check_vma=False,
    )
```

```python
import functools

import jax
import jax.numpy as jnp
from jax import lax
from jax.experimental import pallas as pl
from jax.experimental.pallas import tpu as pltpu
from jax.sharding import PartitionSpec as P

CAP = 64
LANES = 128
PARTS = 2
F32 = jnp.float32
BF16 = jnp.bfloat16

whole = pl.BlockSpec(memory_space=pltpu.VMEM)
scalars = pl.BlockSpec(memory_space=pltpu.SMEM)
outside = pl.BlockSpec(memory_space=pltpu.HBM)


def params(mib=6):
    return pltpu.CompilerParams(vmem_limit_bytes=mib * 2**20)


def slot_source(slot, counts_ref, ranking_ref):
    images = counts_ref.shape[0]
    image, start, end = jnp.int32(0), jnp.int32(0), jnp.int32(0)
    for i in range(images - 1):
        end = end + counts_ref[i]
        past = slot >= end
        image = jnp.where(past, i + 1, image)
        start = jnp.where(past, end, start)
    return image, ranking_ref[image, slot - start]


def gather_kernel(
    counts_any, ranking_any, patches_ref, rows_ref, stats_ref, counts_ref, ranking_ref, sem, sems
):
    copies = [
        pltpu.make_async_copy(counts_any, counts_ref, sems.at[0]),
        pltpu.make_async_copy(ranking_any, ranking_ref, sems.at[1]),
    ]
    for copy in copies:
        copy.start()
    for copy in copies:
        copy.wait()

    def fetch(slot, carry):
        image, patch = slot_source(slot, counts_ref, ranking_ref)
        pltpu.make_async_copy(
            patches_ref.at[image, pl.ds(patch, 1)], rows_ref.at[pl.ds(slot, 1)], sem
        ).start()
        return carry

    lax.fori_loop(0, CAP, fetch, 0, unroll=8)
    pltpu.make_async_copy(patches_ref.at[0, pl.ds(0, CAP)], rows_ref, sem).wait()
    rows = rows_ref[...]
    first = jnp.sum(rows, axis=1, keepdims=True)
    second = jnp.sum(rows * rows, axis=1, keepdims=True)
    lane = lax.broadcasted_iota(jnp.int32, (CAP, LANES), 1)
    stats_ref[...] = jnp.where(lane < LANES // 2, first, second)


def load_kernel(parts, after_ref, *refs):
    weights, refs, sems = refs[: len(parts)], refs[len(parts) : -1], refs[-1]
    copies = []
    for w, part in enumerate(parts):
        share = refs[w].shape[0] // sems.shape[1]
        for i in range(sems.shape[1]):
            row = part * refs[w].shape[0] + i * share
            copies.append(
                pltpu.make_async_copy(
                    weights[w].at[pl.ds(row, share)],
                    refs[w].at[pl.ds(i * share, share)],
                    sems.at[w, i],
                )
            )
    for copy in copies:
        copy.start()
    for copy in copies:
        copy.wait()


def load(after, *shares):
    weights = [weight for weight, _ in shares]
    shapes = [pltpu.VMEM((w.shape[0] // PARTS, w.shape[1]), w.dtype) for w in weights]
    size = sum(w.size * w.dtype.itemsize // PARTS for w in weights)
    loaded = pl.pallas_call(
        functools.partial(load_kernel, tuple(part for _, part in shares)),
        in_specs=[pl.BlockSpec(memory_space=pl.ANY)] + [outside] * len(shares),
        out_specs=[whole] * len(shares),
        out_shape=shapes,
        scratch_shapes=[pltpu.SemaphoreType.DMA((len(shares), 2))],
        compiler_params=params(),
        cost_estimate=pl.CostEstimate(flops=0, bytes_accessed=2 * size, transcendentals=0),
        name="load",
    )(after, *weights)
    return [pltpu.with_memory_space_constraint(w, pltpu.VMEM) for w in loaded]


def copy_kernel(patches_ref, after_ref, out_ref, held_ref, sems):
    images = patches_ref.shape[0]
    inward = [
        pltpu.make_async_copy(patches_ref.at[i], held_ref.at[i], sems.at[0, i])
        for i in range(images)
    ]
    outward = [
        pltpu.make_async_copy(held_ref.at[i], out_ref.at[i], sems.at[1, i]) for i in range(images)
    ]
    for copy in inward:
        copy.start()
    for i in range(images):
        inward[i].wait()
        outward[i].start()
    for copy in outward:
        copy.wait()


def copy(patches, after):
    return pl.pallas_call(
        copy_kernel,
        in_specs=[outside, pl.BlockSpec(memory_space=pl.ANY)],
        out_specs=outside,
        out_shape=pltpu.HBM(patches.shape, patches.dtype),
        scratch_shapes=[
            pltpu.VMEM(patches.shape, patches.dtype),
            pltpu.SemaphoreType.DMA((2, patches.shape[0])),
        ],
        compiler_params=params(),
        cost_estimate=pl.CostEstimate(
            flops=0, bytes_accessed=2 * patches.size * 4, transcendentals=0
        ),
        name="copy",
    )(patches, after)


def pass_kernel(*refs):
    pass


def pass_on(block, after):
    return pl.pallas_call(
        pass_kernel,
        in_specs=[whole] * (1 + len(after)),
        out_specs=whole,
        out_shape=pltpu.VMEM(block.shape, block.dtype),
        input_output_aliases={0: 0},
        compiler_params=params(1),
        name="pass_on",
    )(block, *after)


def norm_kernel(width, rows_ref, gain_ref, after_ref, *refs):
    *stats_refs, out_ref = refs
    stats = stats_refs[0][...]
    for ref in stats_refs[1:]:
        stats = stats + ref[...]
    mean = stats[:, :1] / width
    var = stats[:, LANES - 1 :] / width - mean * mean
    scale = lax.rsqrt(var + 1e-06)
    out_ref[...] = ((rows_ref[...] - mean) * scale * gain_ref[...].reshape(1, -1)).astype(BF16)


def tile_of(width, most):
    return most if width % most == 0 else width


def expand_kernel(first, chunks, groups, last, *refs):
    refs = list(refs)
    weights, refs = refs[:PARTS], refs[PARTS:]
    total_in = refs.pop(0) if first else None
    bias_ref = refs.pop(0) if last else None
    inputs, refs = refs[: chunks * groups], refs[chunks * groups :]
    out_ref, rows_ref = refs[:2]
    total_ref = refs[2] if last else out_ref
    height, width = weights[0].shape[0], rows_ref.shape[1]
    tile = tile_of(height, 256)
    for c in range(chunks):
        for g in range(groups):
            rows_ref[g * CAP : (g + 1) * CAP, :] = inputs[c * groups + g][...]
        column = pl.multiple_of((lax.axis_index("tensor") ^ (first + c)) * width, width)
        for f in range(PARTS * height // tile):
            weight_ref, row = weights[f * tile // height], f * tile % height
            part = lax.dot_general(
                rows_ref[...],
                weight_ref[row : row + tile, pl.ds(column, width)],
                (((1,), (1,)), ((), ())),
                preferred_element_type=F32,
            )
            tiles = slice(f * tile, (f + 1) * tile)
            if c > 0:
                part = part + total_ref[:, tiles]
            elif first:
                part = part + total_in[:, tiles]
            if last and c == chunks - 1:
                pre = part + bias_ref[tiles].reshape(1, -1).astype(F32)
                out_ref[:, tiles] = jax.nn.gelu(pre, approximate=True).astype(BF16)
            else:
                total_ref[:, tiles] = part


def expand(weights, first, total, bias, blocks, groups):
    hidden = PARTS * weights[0].shape[0]
    chunks = len(blocks) // groups
    chunk_width = blocks[0].shape[1]
    rows = groups * CAP
    last = bias is not None
    args = [*weights]
    scratch = [pltpu.VMEM((rows, chunk_width), BF16)]
    if first:
        args.append(total)
    if last:
        args.append(bias)
        scratch.append(pltpu.VMEM((rows, hidden), F32))
    args += blocks
    return pl.pallas_call(
        functools.partial(expand_kernel, first, chunks, groups, last),
        in_specs=[whole] * len(args),
        out_specs=whole,
        out_shape=pltpu.VMEM((rows, hidden), BF16 if last else F32),
        scratch_shapes=scratch,
        compiler_params=params(),
        cost_estimate=pl.CostEstimate(
            flops=2 * rows * hidden * chunk_width * chunks,
            bytes_accessed=2 * rows * chunk_width * chunks,
            transcendentals=0,
        ),
        name="expand",
    )(*args)


def reduce_kernel(groups, start, offset, hidden_ref, *refs):
    weights, refs = refs[:PARTS], refs[PARTS:]
    height, width = weights[0].shape[0], refs[-1].shape[1]
    tile = tile_of(width, 512)
    column = pl.multiple_of((lax.axis_index("tensor") ^ offset) * width, width)
    for n in range(width // tile):
        tiles = slice(n * tile, (n + 1) * tile)
        columns = pl.ds(pl.multiple_of(column + n * tile, LANES), tile)
        part = None
        for i, ref in enumerate(weights):
            term = jnp.dot(
                hidden_ref[start * CAP : (start + groups) * CAP, i * height : (i + 1) * height],
                ref[:, columns],
                preferred_element_type=F32,
            )
            part = term if part is None else part + term
        for g, ref in enumerate(refs[-groups:]):
            piece = part[g * CAP : (g + 1) * CAP]
            if len(refs) > groups:
                piece = piece + refs[g][:, tiles].astype(F32)
            ref[:, tiles] = piece.astype(ref.dtype)


def reduce(hidden, weights, offset, chunks, offsets, received, dtypes):
    groups, depth = len(offsets), hidden.shape[1]
    rows = groups * CAP
    chunk_width = weights[0].shape[1] // chunks
    return pl.pallas_call(
        functools.partial(reduce_kernel, groups, offsets[0], offset),
        in_specs=[whole] * (1 + PARTS + len(received)),
        out_specs=[whole] * groups,
        out_shape=[pltpu.VMEM((CAP, chunk_width), dtype) for dtype in dtypes],
        compiler_params=params(),
        cost_estimate=pl.CostEstimate(
            flops=2 * rows * depth * chunk_width,
            bytes_accessed=2 * rows * chunk_width,
            transcendentals=0,
        ),
        name="reduce",
    )(hidden, *weights, *received)


def add_kernel(*refs):
    *given, out_ref = refs
    value = given[0][...]
    for ref in given[1:]:
        value = value + ref[...].astype(F32)
    out_ref[...] = value.astype(out_ref.dtype)


def add(parts):
    if len(parts) == 1:
        return parts[0]
    return pl.pallas_call(
        add_kernel,
        in_specs=[whole] * len(parts),
        out_specs=whole,
        out_shape=pltpu.VMEM(parts[0].shape, BF16),
        compiler_params=params(4),
        name="add",
    )(*parts)


def scatter_kernel(counts_ref, ranking_ref, rows_ref, bias_ref, patches_ref, own_ref, *refs):
    *received, out_ref, new_ref, sem = refs
    branch = own_ref[...]
    for ref in received:
        branch = branch + ref[...].astype(F32)
    live_slots = counts_ref[0]
    for i in range(1, counts_ref.shape[0]):
        live_slots = live_slots + counts_ref[i]
    slot_index = lax.broadcasted_iota(jnp.int32, branch.shape, 0)
    rows = rows_ref[...]
    new_ref[...] = jnp.where(slot_index < live_slots, rows + (branch + bias_ref[...].reshape(1, -1)), rows)

    def put(slot, carry):
        image, patch = slot_source(slot, counts_ref, ranking_ref)
        pltpu.make_async_copy(
            new_ref.at[pl.ds(slot, 1)], out_ref.at[image, pl.ds(patch, 1)], sem
        ).start()
        return carry

    lax.fori_loop(0, CAP, put, 0, unroll=8)
    pltpu.make_async_copy(new_ref, out_ref.at[0, pl.ds(0, CAP)], sem).wait()


def masks(size):
    return [(2 << k) - 1 for k in reversed(range(size.bit_length() - 1))]


def hops(offset, size, unit, axis):
    path = []
    for mask in masks(size):
        if offset & ((mask + 1) // 2):
            path.append((axis, mask * unit))
            offset ^= mask
    return path


def routes(groups, columns):
    found = {}
    for z in range(groups):
        for y in range(columns):
            along, across = hops(z, groups, 1, "dp"), hops(y, columns, 2, "tensor")
            found[z, y] = tuple(across + along) if z == 1 else tuple(along + across)
    return found


def body(
    sizes, patches, counts, ranking, norm_gain, expand_weight, expand_bias, reduce_weight, reduce_bias
):
    groups, parts = sizes["dp"], sizes["tensor"]
    columns = parts // 2
    images, patch_len, width_local = patches.shape
    width = expand_weight.shape[1]
    patches, counts, ranking, expand_weight, reduce_weight = (
        pltpu.with_memory_space_constraint(a, pltpu.HBM)
        for a in (patches, counts, ranking, expand_weight, reduce_weight)
    )

    def hop(array, axis, mask):
        return lax.ppermute(array, axis, [(i, i ^ mask) for i in range(sizes[axis])])

    rows, stats = pl.pallas_call(
        gather_kernel,
        in_specs=[outside] * 3,
        out_specs=[whole, whole],
        out_shape=[
            pltpu.VMEM((CAP, width_local), F32),
            pltpu.VMEM((CAP, LANES), F32),
        ],
        scratch_shapes=[
            pltpu.SMEM(counts.shape, jnp.int32),
            pltpu.SMEM(ranking.shape, jnp.int32),
            pltpu.SemaphoreType.DMA,
            pltpu.SemaphoreType.DMA((2,)),
        ],
        compiler_params=params(),
        name="gather",
    )(counts, ranking, patches)
    [early] = load(stats, (expand_weight, 0))
    all_stats = [stats] + [hop(stats, "tensor", k) for k in reversed(range(1, parts))]
    normed = pl.pallas_call(
        functools.partial(norm_kernel, width),
        in_specs=[whole] * (3 + parts),
        out_specs=whole,
        out_shape=jax.ShapeDtypeStruct((CAP, width_local), BF16),
        compiler_params=params(),
        name="norm",
    )(rows, norm_gain, early, *all_stats)

    path_of = routes(groups, columns)
    offset_of = {path: offset for offset, path in path_of.items()}
    by_length = sorted((p for p in offset_of if p), key=len)
    late = [(w, i) for w in (expand_weight, reduce_weight) for i in range(1, PARTS)]
    late = load(normed, *late)
    expand_weights = [early] + late[: PARTS - 1]
    half, last = groups // 2, columns - 1
    block = {(): normed}
    far, mid = path_of[groups - 1, 0], path_of[half, 0]
    block[far] = hop(normed, *far[0])
    for path in by_length:
        if len(path) == 1 and path != far:
            block[path] = hop(normed, *path[0])
    near = [block[p] for p in (path_of[0, y] for y in range(1, columns)) if p in block]
    block[far] = pass_on(block[far], late)
    block[mid] = hop(block[far], *mid[-1])
    for y in range(1, columns):
        path = path_of[groups - 1, y]
        if path[:-1] == far:
            block[path] = hop(block[far], *path[-1])
    [reduce_early] = load(block[far], (reduce_weight, 0))
    reduce_weights = [reduce_early] + late[PARTS - 1 :]
    block[mid] = pass_on(
        block[mid],
        [reduce_early] + near + [block[p] for p in by_length if p[:-1] == far and p != mid and p in block],
    )
    for path in by_length:
        if path not in block:
            source = block[path[:-1]]
            if path[-1] == mid[-1]:
                source = pass_on(source, [block[mid]])
            block[path] = hop(source, *path[-1])

    running = None
    for y in range(columns):
        mine = [block[path_of[z, y]] for z in range(groups)]
        if y:
            for z in (1, half):
                mine[z] = pass_on(mine[z], [running])
        inputs = mine + [hop(b, "tensor", 1) for b in mine]
        bias = expand_bias if y == last else None
        running = expand(expand_weights, 2 * y, running, bias, inputs, groups)

    terms = {}
    parents = {p[:-1] for p in by_length}
    for y in reversed(range(columns)):
        ranges = (range(half, groups), range(half))
        received = []
        for offsets in ranges:
            given = reduce(
                running, reduce_weights, 2 * y + 1, parts, offsets, [], [BF16] * half
            )
            received.append([hop(g, "tensor", 1) for g in given])
        for offsets, got in zip(ranges, received):
            paths = [path_of[z, y] for z in offsets]
            dtypes = [F32 if p in parents else BF16 for p in paths]
            kept = reduce(running, reduce_weights, 2 * y, parts, offsets, got, dtypes)
            terms.update((p, [k]) for p, k in zip(paths, kept))
            if y == last and offsets[0]:
                running = pass_on(running, [kept[0]] + [g for b in received for g in b])
    copied = copy(patches, terms[()][0])
    order = list(reversed(by_length))
    for path in order:
        value = add(terms[path])
        if path != order[0] and path[-1] == order[0][-1]:
            value = pass_on(value, [got])
        sent = hop(value, *path[-1])
        if path == order[0]:
            got = sent
        terms[path[:-1]].append(sent)
    own, *arrived = terms[()]

    return pl.pallas_call(
        scatter_kernel,
        in_specs=[scalars, scalars, whole, whole, outside, whole] + [whole] * len(arrived),
        out_specs=outside,
        out_shape=jax.ShapeDtypeStruct(patches.shape, F32),
        scratch_shapes=[pltpu.VMEM((CAP, width_local), F32), pltpu.SemaphoreType.DMA],
        input_output_aliases={4: 0},
        compiler_params=params(),
        name="scatter",
    )(counts, ranking, rows, reduce_bias, copied, own, *arrived)


def solution(mesh):
    placed = (
        P(("groups", "dp"), None, "tensor"),
        P(("groups", "dp")),
        P(("groups", "dp"), None),
        P("tensor"),
        P(("dp", "tensor"), None),
        P(("dp", "tensor")),
        P(("dp", "tensor"), None),
        P("tensor"),
    )
    return jax.shard_map(
        functools.partial(body, dict(mesh.shape)),
        mesh=mesh,
        in_specs=placed,
        out_specs=P(("groups", "dp"), None, "tensor"),
        check_vma=False,
    )
```

```python
import functools

import jax
import jax.numpy as jnp
from jax import lax
from jax.experimental import pallas as pl
from jax.experimental.pallas import tpu as pltpu
from jax.sharding import PartitionSpec as P

CAP = 64
LANES = 128
PARTS = 2
F32 = jnp.float32
BF16 = jnp.bfloat16

whole = pl.BlockSpec(memory_space=pltpu.VMEM)
scalars = pl.BlockSpec(memory_space=pltpu.SMEM)
outside = pl.BlockSpec(memory_space=pltpu.HBM)


def params(mib=6):
    return pltpu.CompilerParams(vmem_limit_bytes=mib * 2**20)


def slot_source(slot, counts_ref, ranking_ref):
    images = counts_ref.shape[0]
    image, start, end = jnp.int32(0), jnp.int32(0), jnp.int32(0)
    for i in range(images - 1):
        end = end + counts_ref[i]
        past = slot >= end
        image = jnp.where(past, i + 1, image)
        start = jnp.where(past, end, start)
    return image, ranking_ref[image, slot - start]


def gather_kernel(
    counts_any, ranking_any, patches_ref, rows_ref, stats_ref, counts_ref, ranking_ref, sem, sems
):
    copies = [
        pltpu.make_async_copy(counts_any, counts_ref, sems.at[0]),
        pltpu.make_async_copy(ranking_any, ranking_ref, sems.at[1]),
    ]
    for copy in copies:
        copy.start()
    for copy in copies:
        copy.wait()

    def fetch(slot, carry):
        image, patch = slot_source(slot, counts_ref, ranking_ref)
        pltpu.make_async_copy(
            patches_ref.at[image, pl.ds(patch, 1)], rows_ref.at[pl.ds(slot, 1)], sem
        ).start()
        return carry

    lax.fori_loop(0, CAP, fetch, 0, unroll=8)
    pltpu.make_async_copy(patches_ref.at[0, pl.ds(0, CAP)], rows_ref, sem).wait()
    rows = rows_ref[...]
    first = jnp.sum(rows, axis=1, keepdims=True)
    second = jnp.sum(rows * rows, axis=1, keepdims=True)
    lane = lax.broadcasted_iota(jnp.int32, (CAP, LANES), 1)
    stats_ref[...] = jnp.where(lane < LANES // 2, first, second)


def load_kernel(parts, after_ref, *refs):
    weights, refs, sems = refs[: len(parts)], refs[len(parts) : -1], refs[-1]
    copies = []
    for w, part in enumerate(parts):
        share = refs[w].shape[0] // sems.shape[1]
        for i in range(sems.shape[1]):
            row = part * refs[w].shape[0] + i * share
            copies.append(
                pltpu.make_async_copy(
                    weights[w].at[pl.ds(row, share)],
                    refs[w].at[pl.ds(i * share, share)],
                    sems.at[w, i],
                )
            )
    for copy in copies:
        copy.start()
    for copy in copies:
        copy.wait()


def load(after, *shares):
    weights = [weight for weight, _ in shares]
    shapes = [pltpu.VMEM((w.shape[0] // PARTS, w.shape[1]), w.dtype) for w in weights]
    size = sum(w.size * w.dtype.itemsize // PARTS for w in weights)
    loaded = pl.pallas_call(
        functools.partial(load_kernel, tuple(part for _, part in shares)),
        in_specs=[pl.BlockSpec(memory_space=pl.ANY)] + [outside] * len(shares),
        out_specs=[whole] * len(shares),
        out_shape=shapes,
        scratch_shapes=[pltpu.SemaphoreType.DMA((len(shares), 2))],
        compiler_params=params(),
        cost_estimate=pl.CostEstimate(flops=0, bytes_accessed=2 * size, transcendentals=0),
        name="load",
    )(after, *weights)
    return [pltpu.with_memory_space_constraint(w, pltpu.VMEM) for w in loaded]


def copy_kernel(patches_ref, after_ref, out_ref, held_ref, sems):
    images = patches_ref.shape[0]
    inward = [
        pltpu.make_async_copy(patches_ref.at[i], held_ref.at[i], sems.at[0, i])
        for i in range(images)
    ]
    outward = [
        pltpu.make_async_copy(held_ref.at[i], out_ref.at[i], sems.at[1, i]) for i in range(images)
    ]
    for copy in inward:
        copy.start()
    for i in range(images):
        inward[i].wait()
        outward[i].start()
    for copy in outward:
        copy.wait()


def copy(patches, after):
    return pl.pallas_call(
        copy_kernel,
        in_specs=[outside, pl.BlockSpec(memory_space=pl.ANY)],
        out_specs=outside,
        out_shape=pltpu.HBM(patches.shape, patches.dtype),
        scratch_shapes=[
            pltpu.VMEM(patches.shape, patches.dtype),
            pltpu.SemaphoreType.DMA((2, patches.shape[0])),
        ],
        compiler_params=params(),
        cost_estimate=pl.CostEstimate(
            flops=0, bytes_accessed=2 * patches.size * 4, transcendentals=0
        ),
        name="copy",
    )(patches, after)


def pass_kernel(*refs):
    pass


def pass_on(block, after):
    return pl.pallas_call(
        pass_kernel,
        in_specs=[whole] * (1 + len(after)),
        out_specs=whole,
        out_shape=pltpu.VMEM(block.shape, block.dtype),
        input_output_aliases={0: 0},
        compiler_params=params(1),
        name="pass_on",
    )(block, *after)


def norm_kernel(width, rows_ref, gain_ref, after_ref, *refs):
    *stats_refs, out_ref = refs
    stats = stats_refs[0][...]
    for ref in stats_refs[1:]:
        stats = stats + ref[...]
    mean = stats[:, :1] / width
    var = stats[:, LANES - 1 :] / width - mean * mean
    scale = lax.rsqrt(var + 1e-06)
    out_ref[...] = ((rows_ref[...] - mean) * scale * gain_ref[...].reshape(1, -1)).astype(BF16)


def tile_of(width, most):
    return most if width % most == 0 else width


def expand_kernel(first, chunks, groups, last, *refs):
    refs = list(refs)
    weights, refs = refs[:PARTS], refs[PARTS:]
    total_in = refs.pop(0) if first else None
    bias_ref = refs.pop(0) if last else None
    inputs, refs = refs[: chunks * groups], refs[chunks * groups :]
    out_ref, rows_ref = refs[:2]
    total_ref = refs[2] if last else out_ref
    height, width = weights[0].shape[0], rows_ref.shape[1]
    tile = tile_of(height, 256)
    for c in range(chunks):
        for g in range(groups):
            rows_ref[g * CAP : (g + 1) * CAP, :] = inputs[c * groups + g][...]
        column = pl.multiple_of((lax.axis_index("tensor") ^ (first + c)) * width, width)
        for f in range(PARTS * height // tile):
            weight_ref, row = weights[f * tile // height], f * tile % height
            part = lax.dot_general(
                rows_ref[...],
                weight_ref[row : row + tile, pl.ds(column, width)],
                (((1,), (1,)), ((), ())),
                preferred_element_type=F32,
            )
            tiles = slice(f * tile, (f + 1) * tile)
            if c > 0:
                part = part + total_ref[:, tiles]
            elif first:
                part = part + total_in[:, tiles]
            if last and c == chunks - 1:
                pre = part + bias_ref[tiles].reshape(1, -1).astype(F32)
                out_ref[:, tiles] = jax.nn.gelu(pre, approximate=True).astype(BF16)
            else:
                total_ref[:, tiles] = part


def expand(weights, first, total, bias, blocks, groups):
    hidden = PARTS * weights[0].shape[0]
    chunks = len(blocks) // groups
    chunk_width = blocks[0].shape[1]
    rows = groups * CAP
    last = bias is not None
    args = [*weights]
    scratch = [pltpu.VMEM((rows, chunk_width), BF16)]
    if first:
        args.append(total)
    if last:
        args.append(bias)
        scratch.append(pltpu.VMEM((rows, hidden), F32))
    args += blocks
    return pl.pallas_call(
        functools.partial(expand_kernel, first, chunks, groups, last),
        in_specs=[whole] * len(args),
        out_specs=whole,
        out_shape=pltpu.VMEM((rows, hidden), BF16 if last else F32),
        scratch_shapes=scratch,
        compiler_params=params(),
        cost_estimate=pl.CostEstimate(
            flops=2 * rows * hidden * chunk_width * chunks,
            bytes_accessed=2 * rows * chunk_width * chunks,
            transcendentals=0,
        ),
        name="expand",
    )(*args)


def reduce_kernel(groups, start, offset, hidden_ref, *refs):
    weights, refs = refs[:PARTS], refs[PARTS:]
    height, width = weights[0].shape[0], refs[-1].shape[1]
    tile = tile_of(width, 512)
    column = pl.multiple_of((lax.axis_index("tensor") ^ offset) * width, width)
    for n in range(width // tile):
        tiles = slice(n * tile, (n + 1) * tile)
        columns = pl.ds(pl.multiple_of(column + n * tile, LANES), tile)
        part = None
        for i, ref in enumerate(weights):
            term = jnp.dot(
                hidden_ref[start * CAP : (start + groups) * CAP, i * height : (i + 1) * height],
                ref[:, columns],
                preferred_element_type=F32,
            )
            part = term if part is None else part + term
        for g, ref in enumerate(refs[-groups:]):
            piece = part[g * CAP : (g + 1) * CAP]
            if len(refs) > groups:
                piece = piece + refs[g][:, tiles].astype(F32)
            ref[:, tiles] = piece.astype(ref.dtype)


def reduce(hidden, weights, offset, chunks, offsets, received, dtypes):
    groups, depth = len(offsets), hidden.shape[1]
    rows = groups * CAP
    chunk_width = weights[0].shape[1] // chunks
    return pl.pallas_call(
        functools.partial(reduce_kernel, groups, offsets[0], offset),
        in_specs=[whole] * (1 + PARTS + len(received)),
        out_specs=[whole] * groups,
        out_shape=[pltpu.VMEM((CAP, chunk_width), dtype) for dtype in dtypes],
        compiler_params=params(),
        cost_estimate=pl.CostEstimate(
            flops=2 * rows * depth * chunk_width,
            bytes_accessed=2 * rows * chunk_width,
            transcendentals=0,
        ),
        name="reduce",
    )(hidden, *weights, *received)


def add_kernel(*refs):
    *given, out_ref = refs
    value = given[0][...]
    for ref in given[1:]:
        value = value + ref[...].astype(F32)
    out_ref[...] = value.astype(out_ref.dtype)


def add(parts):
    if len(parts) == 1:
        return parts[0]
    return pl.pallas_call(
        add_kernel,
        in_specs=[whole] * len(parts),
        out_specs=whole,
        out_shape=pltpu.VMEM(parts[0].shape, BF16),
        compiler_params=params(4),
        name="add",
    )(*parts)


def scatter_kernel(counts_ref, ranking_ref, rows_ref, bias_ref, patches_ref, own_ref, *refs):
    *received, out_ref, new_ref, sem = refs
    branch = own_ref[...]
    for ref in received:
        branch = branch + ref[...].astype(F32)
    live_slots = counts_ref[0]
    for i in range(1, counts_ref.shape[0]):
        live_slots = live_slots + counts_ref[i]
    slot_index = lax.broadcasted_iota(jnp.int32, branch.shape, 0)
    rows = rows_ref[...]
    new_ref[...] = jnp.where(slot_index < live_slots, rows + (branch + bias_ref[...].reshape(1, -1)), rows)

    def put(slot, carry):
        image, patch = slot_source(slot, counts_ref, ranking_ref)
        pltpu.make_async_copy(
            new_ref.at[pl.ds(slot, 1)], out_ref.at[image, pl.ds(patch, 1)], sem
        ).start()
        return carry

    lax.fori_loop(0, CAP, put, 0, unroll=8)
    pltpu.make_async_copy(new_ref, out_ref.at[0, pl.ds(0, CAP)], sem).wait()


def masks(size):
    return [(2 << k) - 1 for k in reversed(range(size.bit_length() - 1))]


def hops(offset, size, unit, axis):
    path = []
    for mask in masks(size):
        if offset & ((mask + 1) // 2):
            path.append((axis, mask * unit))
            offset ^= mask
    return path


def routes(groups, columns):
    found = {}
    for z in range(groups):
        for y in range(columns):
            along, across = hops(z, groups, 1, "dp"), hops(y, columns, 2, "tensor")
            found[z, y] = tuple(across + along) if z == 1 else tuple(along + across)
    return found


def body(
    sizes, patches, counts, ranking, norm_gain, expand_weight, expand_bias, reduce_weight, reduce_bias
):
    groups, parts = sizes["dp"], sizes["tensor"]
    columns = parts // 2
    images, patch_len, width_local = patches.shape
    width = expand_weight.shape[1]
    patches, counts, ranking, expand_weight, reduce_weight = (
        pltpu.with_memory_space_constraint(a, pltpu.HBM)
        for a in (patches, counts, ranking, expand_weight, reduce_weight)
    )

    def hop(array, axis, mask):
        return lax.ppermute(array, axis, [(i, i ^ mask) for i in range(sizes[axis])])

    rows, stats = pl.pallas_call(
        gather_kernel,
        in_specs=[outside] * 3,
        out_specs=[whole, whole],
        out_shape=[
            pltpu.VMEM((CAP, width_local), F32),
            pltpu.VMEM((CAP, LANES), F32),
        ],
        scratch_shapes=[
            pltpu.SMEM(counts.shape, jnp.int32),
            pltpu.SMEM(ranking.shape, jnp.int32),
            pltpu.SemaphoreType.DMA,
            pltpu.SemaphoreType.DMA((2,)),
        ],
        compiler_params=params(),
        name="gather",
    )(counts, ranking, patches)
    [early] = load(stats, (expand_weight, 0))
    all_stats = [stats] + [hop(stats, "tensor", k) for k in reversed(range(1, parts))]
    normed = pl.pallas_call(
        functools.partial(norm_kernel, width),
        in_specs=[whole] * (3 + parts),
        out_specs=whole,
        out_shape=jax.ShapeDtypeStruct((CAP, width_local), BF16),
        compiler_params=params(),
        name="norm",
    )(rows, norm_gain, early, *all_stats)

    path_of = routes(groups, columns)
    offset_of = {path: offset for offset, path in path_of.items()}
    by_length = sorted((p for p in offset_of if p), key=len)
    late = [(w, i) for w in (expand_weight, reduce_weight) for i in range(1, PARTS)]
    late = load(normed, *late)
    expand_weights = [early] + late[: PARTS - 1]
    half, last = groups // 2, columns - 1
    block = {(): normed}
    far, mid = path_of[groups - 1, 0], path_of[half, 0]
    block[far] = hop(normed, *far[0])
    for path in by_length:
        if len(path) == 1 and path != far:
            block[path] = hop(normed, *path[0])
    near = [block[p] for p in (path_of[0, y] for y in range(1, columns)) if p in block]
    block[far] = pass_on(block[far], late)
    block[mid] = hop(block[far], *mid[-1])
    for y in range(1, columns):
        path = path_of[groups - 1, y]
        if path[:-1] == far:
            block[path] = hop(block[far], *path[-1])
    [reduce_early] = load(block[far], (reduce_weight, 0))
    reduce_weights = [reduce_early] + late[PARTS - 1 :]
    block[mid] = pass_on(
        block[mid],
        [reduce_early] + near + [block[p] for p in by_length if p[:-1] == far and p != mid and p in block],
    )
    for path in by_length:
        if path not in block:
            source = block[path[:-1]]
            if path[-1] == mid[-1]:
                source = pass_on(source, [block[mid]])
            block[path] = hop(source, *path[-1])

    running = None
    for y in range(columns):
        mine = [block[path_of[z, y]] for z in range(groups)]
        if y:
            for z in (1, half):
                mine[z] = pass_on(mine[z], [running])
        other = [hop(b, "tensor", 1) for b in mine]
        bias = expand_bias if y == last else None
        if y:
            running = expand(expand_weights, 2 * y, running, None, mine, groups)
            running = expand(expand_weights, 2 * y + 1, running, bias, other, groups)
        else:
            running = expand(expand_weights, 0, running, bias, mine + other, groups)

    terms = {}
    parents = {p[:-1] for p in by_length}
    for y in reversed(range(columns)):
        ranges = (range(half, groups), range(half))
        received = []
        for offsets in ranges:
            given = reduce(
                running, reduce_weights, 2 * y + 1, parts, offsets, [], [BF16] * half
            )
            received.append([hop(g, "tensor", 1) for g in given])
        for offsets, got in zip(ranges, received):
            paths = [path_of[z, y] for z in offsets]
            dtypes = [F32 if p in parents else BF16 for p in paths]
            kept = reduce(running, reduce_weights, 2 * y, parts, offsets, got, dtypes)
            terms.update((p, [k]) for p, k in zip(paths, kept))
            if y == last and offsets[0]:
                running = pass_on(running, [kept[0]] + [g for b in received for g in b])
    copied = copy(patches, terms[()][0])
    order = list(reversed(by_length))
    for path in order:
        value = add(terms[path])
        if path != order[0] and path[-1] == order[0][-1]:
            value = pass_on(value, [got])
        sent = hop(value, *path[-1])
        if path == order[0]:
            got = sent
        terms[path[:-1]].append(sent)
    own, *arrived = terms[()]

    return pl.pallas_call(
        scatter_kernel,
        in_specs=[scalars, scalars, whole, whole, outside, whole] + [whole] * len(arrived),
        out_specs=outside,
        out_shape=jax.ShapeDtypeStruct(patches.shape, F32),
        scratch_shapes=[pltpu.VMEM((CAP, width_local), F32), pltpu.SemaphoreType.DMA],
        input_output_aliases={4: 0},
        compiler_params=params(),
        name="scatter",
    )(counts, ranking, rows, reduce_bias, copied, own, *arrived)


def solution(mesh):
    placed = (
        P(("groups", "dp"), None, "tensor"),
        P(("groups", "dp")),
        P(("groups", "dp"), None),
        P("tensor"),
        P(("dp", "tensor"), None),
        P(("dp", "tensor")),
        P(("dp", "tensor"), None),
        P("tensor"),
    )
    return jax.shard_map(
        functools.partial(body, dict(mesh.shape)),
        mesh=mesh,
        in_specs=placed,
        out_specs=P(("groups", "dp"), None, "tensor"),
        check_vma=False,
    )
```
